32 devices in a mesh: group: 2 (over y), expert: 4 (over z), tensor: 4 (over x, core).
Axes of the slice: x: 2, y: 2, z: 4, core: 2. Of those that a mesh axis runs over, the one named last changes fastest.
Arguments:
- tokens: bfloat16 [2048, 4096], P(('group', 'expert', 'tensor')), parts along dimension 0, may hold values from -6 to 6
- expert_ids: int32 [2048, 8], P(('group', 'expert', 'tensor')), parts along dimension 0, may hold values from 0 to 7, all different within a row; in each aligned block of 64 rows (0 to 63, 64 to 127, ...) at most 64 rows name the same one
- gate_weights: float32 [2048, 8], P(('group', 'expert', 'tensor')), parts along dimension 0, may hold values from 0.05 to 1
- w_gate: bfloat16 [16, 4096, 384], P(('expert', 'tensor')), may hold values from -0.09375 to 0.09375
- w_up: bfloat16 [16, 4096, 384], P(('expert', 'tensor')), may hold values from -0.09375 to 0.09375
- w_down: bfloat16 [16, 384, 4096], P(('expert', 'tensor')), may hold values from -0.21875 to 0.21875
Outputs:
- combined: bfloat16 [2048, 4096], P(('group', 'expert', 'tensor')), parts along dimension 0
The draws below stay inside these ranges and needn't reach their ends.
There are 2 independent parts, one for each index of `group`. The reference program is written for one: setup_inputs(seed, part) draws one part's arguments, and reference() takes and returns one part's arrays. A program takes and returns all parts, laid end to end along the dimension named above; an argument that names none is the same for every part. Nothing has to cross between parts.
Inputs may be any that keep to these rules, and one draw needn't show every extreme that they name: `expert_ids`: each row names 8 different experts. Among the 64 rows of one device, no expert is named by more than 64 rows, a bound that some block reaches.
All inputs are finite; a program needn't handle non-finite values. Where the reference program divides by a largest or mean magnitude, that divisor is 1e-20 or more.
Results may differ from the reference program's by a relative error of at most 0.03.
Values may be sent and summed in bfloat16 or wider, within the bound.
A program may use at most 128 MiB of HBM per device.

```python
import math
import jax
import jax.numpy as jnp
import numpy as np
from jax import lax

D = 4096
FF = 768
TOPK = 8
ROT = 128
TOK_DEV = 64
EXPERTS = 8
CAP = 64
TOKENS = 1024
N_EXPERT = 4
N_TENSOR = 4


def shard_levels(stream_key, dims, pieces, smallest, high):
    def one(dim, shards_of):
        heights = jax.random.uniform(jax.random.fold_in(jax.random.fold_in(stream_key, 6), dim), (shards_of,), jnp.float32, smallest / len(pieces), high / len(pieces))
        return jnp.repeat(jnp.exp(heights), dims[dim] // shards_of).reshape((-1,) + (1,) * (len(dims) - dim - 1))

    loudness = one(*pieces[0])
    for cut in pieces[1:]:
        loudness = loudness * one(*cut)
    return loudness


def deal_out(rng, own, number, rows, amount, top, limit, lean):
    sequence = jax.random.permutation(rng, amount)
    packed, usual = load_shares(amount, rows * top, limit, lean, True), load_shares(amount, rows * top, limit, lean, False)
    places = jnp.arange(amount)

    def named(tallies, offset_by):
        used = int((tallies > 0).sum())
        fixed = max(1, used // 4)
        passed = fixed + (places - fixed + offset_by * (used - fixed)) % max(1, amount - fixed)
        return jnp.zeros((amount,), jnp.int32).at[sequence[jnp.where(places < fixed, places, passed)]].set(jnp.asarray(tallies, jnp.int32))

    tallies = jnp.where(number % 4 == 0, named(packed, number // 4), named(usual, number - number // 4 - 1))
    mixed = jax.random.permutation(jax.random.fold_in(own, 3), amount)
    donor, taker = mixed[0:amount // 2 * 2:2], mixed[1:amount // 2 * 2:2]
    room = jnp.minimum(tallies[donor] - 1, limit - tallies[taker]) // 2
    room = jnp.where((donor == sequence[0]) | (taker == sequence[0]) | (tallies[taker] == 0), 0, jnp.maximum(room, 0))
    passed = jax.random.randint(jax.random.fold_in(own, 4), (amount // 2,), 0, 1 << 20) % (room + 1)
    tallies = tallies.at[donor].add(-passed).at[taker].add(passed)
    members = jnp.searchsorted(jnp.cumsum(tallies), jnp.arange(rows * top), side="right").astype(jnp.int32)
    grid = members.reshape(top, rows).T
    grid = grid[jax.random.permutation(jax.random.fold_in(own, 1), rows)]
    offset_by = jax.random.randint(jax.random.fold_in(own, 2), (rows, 1), 0, top)
    return jnp.take_along_axis(grid, (jnp.arange(top)[None, :] + offset_by) % top, axis=1)


def load_shares(count, total, limit, skew, full):
    portions = [(1 << 20) // math.isqrt(rank ** skew) + 1 for rank in range(1, count + 1)]
    largest = limit if full else min(limit, max(-(-total // count), total * portions[0] // sum(portions)))
    least = 1 if total - largest >= count - 1 else 0
    counts, surplus = [largest] + [least] * (count - 1), total - largest - least * (count - 1)
    while surplus > 0:
        movable = [i for i in range(1, count) if counts[i] < largest] or [i for i in range(1, count) if counts[i] < limit]
        whole, remaining = sum([portions[i] for i in movable]), surplus
        for i in movable:
            addition = min(limit - counts[i], max(1, remaining * portions[i] // whole), surplus)
            counts[i] = counts[i] + addition
            surplus = surplus - addition
    return np.array(counts)


def scatter_about(stream_key, extent, spread, most, split=(), kind=jnp.bfloat16):
    gain = shard_levels(stream_key, extent, split, -0.22, 0.18) if split else 1.0
    entries = jax.random.normal(stream_key, extent, jnp.float32) * spread * gain
    return jnp.minimum(jnp.maximum(entries, -most), most).astype(kind)


def setup_inputs(seed: int = 0, part: int = 0) -> dict:
    key_list = jax.random.split(jax.random.key(seed), 7)
    part_keys = jax.random.split(jax.random.fold_in(key_list[6], part), 7)
    tokens = scatter_about(part_keys[0], (TOKENS, D), 1.0, 6.0, ((0, 16),))
    expert_ids_keys = jax.random.split(jax.random.fold_in(part_keys[1], 1), TOKENS // TOK_DEV)
    expert_ids_turns = jax.random.permutation(jax.random.fold_in(part_keys[1], 3), TOKENS // TOK_DEV)
    expert_ids = jax.vmap(lambda own, number: deal_out(jax.random.fold_in(part_keys[1], 2), own, number, TOK_DEV, EXPERTS, TOPK, CAP, 2))(expert_ids_keys, expert_ids_turns).reshape((TOKENS, TOPK))
    gate_weights = jnp.clip(jnp.exp(math.log(1.0) - 2.9957323 * jax.random.uniform(part_keys[2], (TOKENS, TOPK), jnp.float32) ** shard_levels(part_keys[2], (TOKENS, TOPK), ((0, 16),), -0.2, 0.2)), 0.05, 1.0)
    w_gate = scatter_about(key_list[3], (2 * EXPERTS, D, FF // 2), D ** -0.5, 0.09375, ((0, 16),))
    w_up = scatter_about(key_list[4], (2 * EXPERTS, D, FF // 2), D ** -0.5, 0.09375, ((0, 16),))
    w_down = scatter_about(key_list[5], (2 * EXPERTS, FF // 2, D), FF ** -0.5, 0.21875, ((0, 16),))
    return dict(tokens=tokens, expert_ids=expert_ids, gate_weights=gate_weights, w_gate=w_gate, w_up=w_up, w_down=w_down)


def hadamard():
    position = lax.iota(jnp.int32, ROT)
    common_bits = jnp.bitwise_and(position[:, None], position[None, :])
    parity = jnp.zeros((ROT, ROT), jnp.int32)
    for bit_index in range(ROT.bit_length() - 1):
        parity = parity + jnp.bitwise_and(jnp.right_shift(common_bits, bit_index), 1)
    return (1 - 2 * (parity % 2)).astype(jnp.float32) / math.sqrt(ROT)

def rotate(values, hadamard_table):
    blocks = values.reshape(values.shape[0], -1, ROT)
    turned = jnp.einsum('rbi,ij->rbj', blocks, hadamard_table, precision=lax.Precision.HIGHEST)
    return turned.reshape(values.shape)

def reference(tokens, expert_ids, gate_weights, w_gate, w_up, w_down):
    hadamard_table = hadamard()
    devices = N_EXPERT * N_TENSOR
    per_device = expert_ids.reshape(devices, TOK_DEV * TOPK)
    onehot = (per_device[:, :, None] == jnp.arange(EXPERTS, dtype=jnp.int32)[None, None, :]).astype(jnp.int32)
    before = jnp.cumsum(onehot, axis=1, dtype=jnp.int32) - onehot
    slot_index = lax.optimization_barrier(jnp.sum(before * onehot, axis=-1)).astype(jnp.int32)
    place = (jnp.arange(devices, dtype=jnp.int32)[:, None] * CAP + slot_index).reshape(-1)
    flat_ids = expert_ids.reshape(-1).astype(jnp.int32)
    token_of = (jnp.arange(TOKENS * TOPK, dtype=jnp.int32) // TOPK).astype(jnp.int32)
    row_table = jnp.full((EXPERTS, devices * CAP), TOKENS, jnp.int32).at[flat_ids, place].set(token_of)
    weight_table = jnp.zeros((EXPERTS, devices * CAP), jnp.float32).at[flat_ids, place].set(gate_weights.reshape(-1).astype(jnp.float32))
    padded = jnp.concatenate([tokens, jnp.zeros((1, D), tokens.dtype)], axis=0)

    def expert_step(accumulated, expert):
        picked = padded[row_table[expert]]
        output = jnp.zeros((devices * CAP, D), jnp.float32)
        for which in range(2):
            row_index = 2 * expert + which
            gate_proj = jnp.dot(picked, w_gate[row_index], preferred_element_type=jnp.float32)
            up_proj = jnp.dot(picked, w_up[row_index], preferred_element_type=jnp.float32)
            hidden = (jax.nn.silu(gate_proj) * up_proj).astype(jnp.bfloat16)
            output = output + jnp.dot(hidden, w_down[row_index], preferred_element_type=jnp.float32)
        rotated = rotate(output, hadamard_table).reshape(devices * CAP, D // ROT, ROT)
        scales = lax.optimization_barrier(jnp.max(jnp.abs(rotated), axis=-1, keepdims=True)) + 1e-06
        quantized = lax.optimization_barrier((rotated / scales + 3.0).astype(jnp.bfloat16))
        restored = ((quantized.astype(jnp.float32) - 3.0) * scales).reshape(devices * CAP, D)
        accumulated = accumulated.at[row_table[expert]].add(weight_table[expert][:, None] * restored)
        return (accumulated, None)
    accumulated, unused = lax.scan(expert_step, jnp.zeros((TOKENS + 1, D), jnp.float32), jnp.arange(EXPERTS, dtype=jnp.int32))
    return rotate(accumulated[:TOKENS], hadamard_table).astype(jnp.bfloat16)
```

```python
import math

import jax
import jax.numpy as jnp
from jax import lax
from jax.experimental import pallas as pl
from jax.experimental.pallas import tpu as pltpu
from jax.sharding import PartitionSpec as P

ROT = 128


def swapped(value, axis, apart):
    mask = 2**apart
    pairs = [(source, source ^ mask) for source in range(lax.axis_size(axis))]
    return lax.ppermute(value, axis, pairs)


def hadamard():
    position = lax.iota(jnp.int32, ROT)
    common_bits = jnp.bitwise_and(position[:, None], position[None, :])
    parity = jnp.zeros((ROT, ROT), jnp.int32)
    for bit_index in range(ROT.bit_length() - 1):
        parity = parity + jnp.bitwise_and(jnp.right_shift(common_bits, bit_index), 1)
    return (1 - 2 * (parity % 2)).astype(jnp.float32) / math.sqrt(ROT)


def rotate(values, hadamard_table):
    blocks = values.reshape(values.shape[0], -1, ROT)
    turned = jnp.einsum("rbi,ij->rbj", blocks, hadamard_table, precision=lax.Precision.HIGHEST)
    return turned.reshape(values.shape)


def ring_kernel(
    tokens_ref, ids_ref, gains_ref, gate_ref, up_ref, down_ref, out_ref,
    tok, wg, wu, wd_raw, wd, mine, exch_send, exch_recv, rs_send, rs_recv, fin_send, fin_recv,
    load_sem, tok_send_sem, tok_recv_sem, pair_send_sem, pair_recv_sem,
    exch_send_sem, exch_recv_sem, rs_send_sem, rs_recv_sem, fin_sem,
):
    slots, _, rows, _ = tok.shape
    half_rows = rows // 2
    width = tokens_ref.shape[1]
    half = width // 2
    last = slots - 1

    group = lax.axis_index("group")
    along_z = lax.axis_index("expert")
    tensor = lax.axis_index("tensor")
    core = lax.rem(tensor, 2)
    along_x = tensor // 2
    length = slots // 2
    expert = along_z * 2 + along_x
    position = jnp.where(along_x == 0, along_z, slots - 1 - along_z)

    def device_at(place):
        place = lax.rem(place + slots, slots)
        x = place // length
        z = jnp.where(x == 0, place, slots - 1 - place)
        return (group, z, 2 * x + core)

    neighbours = (device_at(position + 1), device_at(position - 1))
    partner = (group, along_z, 2 * along_x + 1 - core)

    def remote(src, dst, send, recv, device):
        return pltpu.make_async_remote_copy(
            src_ref=src, dst_ref=dst, send_sem=send, recv_sem=recv,
            device_id=device, device_id_type=pl.DeviceIdType.MESH,
        )

    def tok_copy(s, way):
        part = pl.ds(way * half_rows, half_rows)
        return remote(
            tok.at[s, 0, part], tok.at[s + 1, 0, part],
            tok_send_sem.at[way, s], tok_recv_sem.at[way, s + 1], neighbours[way],
        )

    def pair_copy(s):
        return remote(tok.at[s, 0], tok.at[s, 1], pair_send_sem.at[s], pair_recv_sem.at[s], partner)

    def exch_copy(s):
        return remote(
            exch_send.at[s], exch_recv.at[s], exch_send_sem.at[s], exch_recv_sem.at[s], partner
        )

    def rs_copy(s, way):
        return remote(
            rs_send.at[s, way], rs_recv.at[s + 1, way],
            rs_send_sem.at[way, s], rs_recv_sem.at[way, s + 1], neighbours[way],
        )

    barrier = pltpu.get_barrier_semaphore()
    for device in (*neighbours, partner):
        pl.semaphore_signal(barrier, inc=1, device_id=device, device_id_type=pl.DeviceIdType.MESH)

    loads = [
        pltpu.make_async_copy(tokens_ref, tok.at[0, 0, :, pl.ds(0, width)], load_sem.at[0]),
        pltpu.make_async_copy(down_ref.at[0], wd_raw, load_sem.at[1]),
        pltpu.make_async_copy(gate_ref.at[0], wg, load_sem.at[2]),
        pltpu.make_async_copy(up_ref.at[0], wu, load_sem.at[3]),
    ]
    for load in loads:
        load.start()

    lane = lax.broadcasted_iota(jnp.int32, (rows, ROT), 1)
    lane_expert = lax.rem(lane, slots)
    lane_term = lane // slots
    weight = jnp.zeros((rows, ROT), jnp.float32)
    for k in range(ids_ref.shape[1]):
        weight = weight + jnp.where(ids_ref[:, k : k + 1] == lane_expert, gains_ref[:, k : k + 1], 0.0)
    first = weight.astype(jnp.bfloat16).astype(jnp.float32)
    second = (weight - first).astype(jnp.bfloat16).astype(jnp.float32)
    third = weight - first - second
    packed = jnp.where(
        lane_term == 0, first, jnp.where(lane_term == 1, second, jnp.where(lane_term == 2, third, 0.0))
    )
    tok[0, 0, :, width:] = packed.astype(jnp.bfloat16)

    loads[0].wait()
    pl.semaphore_wait(barrier, 3)
    tok_copy(0, 0).start()
    tok_copy(0, 1).start()
    pair_copy(0).start()

    rs_recv[0] = jnp.zeros(rs_recv.shape[1:], rs_recv.dtype)
    rs_recv[1] = jnp.zeros(rs_recv.shape[1:], rs_recv.dtype)

    bits = lax.broadcasted_iota(jnp.int32, (ROT, ROT), 0) & lax.broadcasted_iota(jnp.int32, (ROT, ROT), 1)
    bits = bits ^ (bits >> 4)
    bits = bits ^ (bits >> 2)
    bits = (bits ^ (bits >> 1)) & 1
    signs = (1 - 2 * bits).astype(jnp.float32).astype(jnp.bfloat16)
    norm = 1.0 / math.sqrt(ROT)

    loads[1].wait()
    for which in range(2):
        start = jnp.where(which == 0, core, 1 - core) * half
        for block in range(half // ROT):
            columns = pl.ds(pl.multiple_of(start + block * ROT, ROT), ROT)
            turned = jnp.dot(wd_raw[:, columns], signs, preferred_element_type=jnp.float32) * norm
            wd[which, :, block * ROT : (block + 1) * ROT] = turned.astype(jnp.bfloat16)
    loads[2].wait()
    loads[3].wait()

    def step(s, carry):
        @pl.when(s >= 1)
        def _():
            tok_copy(s - 1, 0).wait_recv()
            tok_copy(s - 1, 1).wait_recv()

            @pl.when(s < last)
            def _():
                tok_copy(s, 0).start()
                tok_copy(s, 1).start()

            pair_copy(s).start()

        pair_copy(s).wait_recv()
        x = tok[s, :, :, :width].reshape(2 * rows, width)
        gate = jnp.dot(x, wg[...], preferred_element_type=jnp.float32)
        up = jnp.dot(x, wu[...], preferred_element_type=jnp.float32)
        hidden = (gate / (1.0 + jnp.exp(-gate)) * up).astype(jnp.bfloat16)
        theirs = jnp.dot(hidden, wd[1], preferred_element_type=jnp.float32).astype(jnp.bfloat16)
        exch_send[s, :rows] = theirs[rows:]
        exch_send[s, rows:] = theirs[:rows]
        exch_copy(s).start()
        mine[...] = jnp.dot(hidden, wd[0], preferred_element_type=jnp.float32)
        tail = tok[s, :, :, width:].reshape(2 * rows, ROT).astype(jnp.float32)
        wide = lax.broadcasted_iota(jnp.int32, (2 * rows, ROT), 1)
        gain = jnp.sum(jnp.where(lax.rem(wide, slots) == expert, tail, 0.0), axis=1, keepdims=True)
        exch_copy(s).wait_recv()

        @pl.when(s >= 2)
        def _():
            rs_copy(s - 1, 0).wait_recv()
            rs_copy(s - 1, 1).wait_recv()

        for block in range(half // ROT):
            columns = slice(block * ROT, (block + 1) * ROT)
            value = mine[:, columns] + exch_recv[s, :, columns].astype(jnp.float32)
            scale = jnp.max(jnp.abs(value), axis=1, keepdims=True) + 1e-06
            quantized = (value * (1.0 / scale) + 3.0).astype(jnp.bfloat16)
            restored = (quantized.astype(jnp.float32) - 3.0) * (scale * gain)
            for way in range(2):
                for which in range(2):
                    top = which * rows + way * half_rows
                    total = restored[top : top + half_rows] + rs_recv[s, way, which, :, columns].astype(
                        jnp.float32
                    )
                    rs_send[s, way, which, :, columns] = total.astype(jnp.bfloat16)

        @pl.when(s >= 1)
        def _():
            rs_copy(s, 0).start()
            rs_copy(s, 1).start()

        return carry

    lax.fori_loop(0, slots, step, 0)

    rs_copy(last, 0).wait_recv()
    rs_copy(last, 1).wait_recv()
    doubled = jnp.concatenate([signs, signs], axis=0)
    for which in (1, 0):
        for block in range(half // ROT):
            columns = slice(block * ROT, (block + 1) * ROT)
            pieces = [
                rs_send[0, way, which, :, columns].astype(jnp.float32)
                + rs_recv[slots, way, which, :, columns].astype(jnp.float32)
                for way in range(2)
            ]
            total = jnp.concatenate(pieces, axis=0)
            high = total.astype(jnp.bfloat16)
            low = (total - high.astype(jnp.float32)).astype(jnp.bfloat16)
            turned = jnp.dot(
                jnp.concatenate([high, low], axis=1), doubled, preferred_element_type=jnp.float32
            )
            result = (turned * norm).astype(jnp.bfloat16)
            if which == 1:
                fin_send[:, columns] = result
            else:
                out_ref[:, pl.ds(pl.multiple_of(core * half + block * ROT, ROT), ROT)] = result
        if which == 1:
            fin_copy = remote(fin_send, fin_recv, fin_sem.at[0], fin_sem.at[1], partner)
            fin_copy.start()

    def drain(s, carry):
        pair_copy(s).wait_send()
        exch_copy(s).wait_send()
        for way in range(2):
            @pl.when(s < last)
            def _():
                tok_copy(s, way).wait_send()

            @pl.when(s >= 1)
            def _():
                rs_copy(s, way).wait_send()
        return carry

    lax.fori_loop(0, slots, drain, 0)
    fin_copy.wait_recv()
    out_ref[:, pl.ds(pl.multiple_of((1 - core) * half, half), half)] = fin_recv[...]
    fin_copy.wait_send()


def ring_layer(tokens, expert_ids, gate_weights, w_gate, w_up, w_down):
    rows, width = tokens.shape
    hidden = w_gate.shape[2]
    half = width // 2
    slots = 2 * lax.axis_size("expert")
    dma, bf16 = pltpu.SemaphoreType.DMA, jnp.bfloat16
    anywhere = pl.BlockSpec(memory_space=pl.ANY)
    vmem = pl.BlockSpec(memory_space=pltpu.VMEM)
    return pl.pallas_call(
        ring_kernel,
        out_shape=jax.ShapeDtypeStruct((rows, width), bf16),
        in_specs=[anywhere, vmem, vmem, anywhere, anywhere, anywhere],
        out_specs=vmem,
        scratch_shapes=[
            pltpu.VMEM((slots, 2, rows, width + ROT), bf16),
            pltpu.VMEM((width, hidden), bf16),
            pltpu.VMEM((width, hidden), bf16),
            pltpu.VMEM((hidden, width), bf16),
            pltpu.VMEM((2, hidden, half), bf16),
            pltpu.VMEM((2 * rows, half), jnp.float32),
            pltpu.VMEM((slots, 2 * rows, half), bf16),
            pltpu.VMEM((slots, 2 * rows, half), bf16),
            pltpu.VMEM((slots, 2, 2, rows // 2, half), bf16),
            pltpu.VMEM((slots + 1, 2, 2, rows // 2, half), bf16),
            pltpu.VMEM((rows, half), bf16),
            pltpu.VMEM((rows, half), bf16),
            dma((4,)),
            dma((2, slots)),
            dma((2, slots)),
            dma((slots,)),
            dma((slots,)),
            dma((slots,)),
            dma((slots,)),
            dma((2, slots)),
            dma((2, slots + 1)),
            dma((2,)),
        ],
        compiler_params=pltpu.CompilerParams(
            collective_id=0, has_side_effects=True, vmem_limit_bytes=56 * 1024 * 1024
        ),
    )(tokens, expert_ids, gate_weights, w_gate, w_up, w_down)


def local(tokens, expert_ids, gate_weights, w_gate, w_up, w_down):
    hadamard_table = hadamard()
    tok_rows, model_width = tokens.shape
    top_count = expert_ids.shape[1]
    n_expert = lax.axis_size("expert")
    n_tensor = lax.axis_size("tensor")
    devices = n_expert * n_tensor
    experts = devices // 2
    capacity = max(2, min(tok_rows, 5 * tok_rows * top_count // (4 * experts)))
    if capacity == tok_rows and n_tensor == 4 and experts == 2 * n_expert and experts * 3 <= ROT:
        return ring_layer(tokens, expert_ids, gate_weights, w_gate, w_up, w_down)
    half_width = model_width // 2
    my_half = lax.axis_index("tensor") % 2
    gate_mat = w_gate[0]
    up_mat = w_up[0]
    down_mat = w_down[0]
    flat_ids = expert_ids.reshape(-1)
    onehot = (flat_ids[:, None] == lax.iota(jnp.int32, experts)[None, :]).astype(jnp.int32)
    slot_index = jnp.sum((jnp.cumsum(onehot, axis=0, dtype=jnp.int32) - onehot) * onehot, axis=1)
    lower_row = 2 * flat_ids * capacity + slot_index
    upper_row = lower_row + capacity
    copies = tokens[lax.iota(jnp.int32, tok_rows * top_count) // top_count]
    both_rows = jnp.concatenate([lower_row, upper_row])
    outgoing = jnp.zeros((devices * capacity, model_width), jnp.bfloat16)
    outgoing = outgoing.at[both_rows].set(jnp.concatenate([copies, copies], axis=0))
    received = lax.all_to_all(
        outgoing.reshape(devices, capacity, model_width),
        ("expert", "tensor"),
        split_axis=0,
        concat_axis=0,
        tiled=True,
    )
    token_rows = received.reshape(-1, model_width)
    item_count = received.shape[1]
    gate_proj = jnp.dot(token_rows, gate_mat, preferred_element_type=jnp.float32)
    up_proj = jnp.dot(token_rows, up_mat, preferred_element_type=jnp.float32)
    hidden = (jax.nn.silu(gate_proj) * up_proj).astype(jnp.bfloat16)
    partial_out = jnp.dot(hidden, down_mat, preferred_element_type=jnp.float32)
    own_part = lax.dynamic_slice_in_dim(partial_out, my_half * half_width, half_width, 1)
    other_part = lax.dynamic_slice_in_dim(partial_out, (1 - my_half) * half_width, half_width, 1)
    partner_part = swapped(other_part.astype(jnp.bfloat16), "tensor", 0).astype(other_part.dtype)
    summed = own_part + partner_part
    rotated = rotate(summed, hadamard_table).reshape(-1, half_width // ROT, ROT)
    scales = jnp.max(jnp.abs(rotated), axis=-1) + 1e-06
    quantized = (rotated / scales[:, :, None] + 3.0).astype(jnp.bfloat16)
    quant_out = quantized.reshape(devices, item_count, half_width)
    scale_out = scales.reshape(devices, item_count, half_width // ROT)
    back_quant, back_scales = (
        lax.all_to_all(quant_out, ("expert", "tensor"), split_axis=0, concat_axis=0, tiled=True),
        lax.all_to_all(
            scale_out.astype(jnp.bfloat16),
            ("expert", "tensor"),
            split_axis=0,
            concat_axis=0,
            tiled=True,
        ).astype(scale_out.dtype),
    )
    flat_quant = back_quant.reshape(devices * capacity, half_width // ROT, ROT)
    flat_scales = back_scales.reshape(devices * capacity, half_width // ROT)

    def restore(row_index):
        picked = (flat_quant[row_index].astype(jnp.float32) - 3.0) * flat_scales[row_index][
            :, :, None
        ]
        return picked.reshape(-1, half_width)

    restored = jnp.concatenate([restore(lower_row), restore(upper_row)], axis=1)
    mixed = jnp.einsum(
        "tkd,tk->td",
        restored.reshape(tok_rows, top_count, model_width),
        gate_weights,
        precision=lax.Precision.HIGHEST,
    )
    return rotate(mixed, hadamard_table).astype(jnp.bfloat16)


def solution(mesh):
    in_specs = (
        P(("group", "expert", "tensor"), None),
        P(("group", "expert", "tensor"), None),
        P(("group", "expert", "tensor"), None),
        P(("expert", "tensor"), None, None),
        P(("expert", "tensor"), None, None),
        P(("expert", "tensor"), None, None),
    )
    out_specs = P(("group", "expert", "tensor"), None)
    return jax.shard_map(local, mesh=mesh, in_specs=in_specs, out_specs=out_specs, check_vma=False)
```

```python
import math

import jax
import jax.numpy as jnp
from jax import lax
from jax.experimental import pallas as pl
from jax.experimental.pallas import tpu as pltpu
from jax.sharding import PartitionSpec as P

ROT = 128


def swapped(value, axis, apart):
    mask = 2**apart
    pairs = [(source, source ^ mask) for source in range(lax.axis_size(axis))]
    return lax.ppermute(value, axis, pairs)


def hadamard():
    position = lax.iota(jnp.int32, ROT)
    common_bits = jnp.bitwise_and(position[:, None], position[None, :])
    parity = jnp.zeros((ROT, ROT), jnp.int32)
    for bit_index in range(ROT.bit_length() - 1):
        parity = parity + jnp.bitwise_and(jnp.right_shift(common_bits, bit_index), 1)
    return (1 - 2 * (parity % 2)).astype(jnp.float32) / math.sqrt(ROT)


def rotate(values, hadamard_table):
    blocks = values.reshape(values.shape[0], -1, ROT)
    turned = jnp.einsum("rbi,ij->rbj", blocks, hadamard_table, precision=lax.Precision.HIGHEST)
    return turned.reshape(values.shape)


PIECES = 2


def ring_kernel(
    tokens_ref, ids_ref, gains_ref, gate_ref, up_ref, down_ref, out_ref,
    tok, wg, wu, wd_raw, wd, mine, exch_send, exch_recv, rs_send, rs_recv, fin_send, fin_recv,
    ids, gains, load_sem, tok_send_sem, tok_recv_sem, pair_send_sem, pair_recv_sem,
    exch_send_sem, exch_recv_sem, rs_send_sem, rs_recv_sem, fin_sem,
):
    slots, _, rows, _ = tok.shape
    half_rows = rows // 2
    width = tokens_ref.shape[1]
    half = width // 2
    last = slots - 1
    pieces, part = rs_send.shape[2], rs_send.shape[5]

    group = lax.axis_index("group")
    along_z = lax.axis_index("expert")
    tensor = lax.axis_index("tensor")
    core = lax.rem(tensor, 2)
    along_x = tensor // 2
    length = slots // 2
    expert = along_z * 2 + along_x
    position = jnp.where(along_x == 0, along_z, slots - 1 - along_z)

    def device_at(place):
        place = lax.rem(place + slots, slots)
        x = place // length
        z = jnp.where(x == 0, place, slots - 1 - place)
        return (group, z, 2 * x + core)

    neighbours = (device_at(position + 1), device_at(position - 1))
    partner = (group, along_z, 2 * along_x + 1 - core)

    def remote(src, dst, send, recv, device):
        return pltpu.make_async_remote_copy(
            src_ref=src, dst_ref=dst, send_sem=send, recv_sem=recv,
            device_id=device, device_id_type=pl.DeviceIdType.MESH,
        )

    def tok_copy(s, way):
        mine_way = pl.ds(way * half_rows, half_rows)
        return remote(
            tok.at[s, 0, mine_way], tok.at[s + 1, 0, mine_way],
            tok_send_sem.at[way, s], tok_recv_sem.at[way, s + 1], neighbours[way],
        )

    def pair_copy(s):
        return remote(tok.at[s, 0], tok.at[s, 1], pair_send_sem.at[s], pair_recv_sem.at[s], partner)

    def exch_copy(s):
        return remote(
            exch_send.at[s], exch_recv.at[s], exch_send_sem.at[s], exch_recv_sem.at[s], partner
        )

    def rs_copy(s, way, piece):
        return remote(
            rs_send.at[s, way, piece], rs_recv.at[s + 1, way, piece],
            rs_send_sem.at[way, piece, s], rs_recv_sem.at[way, piece, s + 1], neighbours[way],
        )

    def fin_copy(piece):
        return remote(
            fin_send.at[piece], fin_recv.at[piece], fin_sem.at[0, piece], fin_sem.at[1, piece], partner
        )

    barrier = pltpu.get_barrier_semaphore()
    for device in (*neighbours, partner):
        pl.semaphore_signal(barrier, inc=1, device_id=device, device_id_type=pl.DeviceIdType.MESH)

    loads = [
        pltpu.make_async_copy(tokens_ref, tok.at[0, 0, :, pl.ds(0, width)], load_sem.at[0]),
        pltpu.make_async_copy(down_ref.at[0], wd_raw, load_sem.at[1]),
        pltpu.make_async_copy(gate_ref.at[0], wg, load_sem.at[2]),
        pltpu.make_async_copy(up_ref.at[0], wu, load_sem.at[3]),
        pltpu.make_async_copy(ids_ref, ids, load_sem.at[4]),
        pltpu.make_async_copy(gains_ref, gains, load_sem.at[5]),
    ]
    loads = loads[4:] + loads[:4]
    for load in loads:
        load.start()

    loads[0].wait()
    loads[1].wait()
    place = lax.broadcasted_iota(jnp.int32, (ROT, rows), 0)
    place_expert = lax.rem(place, slots)
    place_term = place // slots
    weight = jnp.zeros((ROT, rows), jnp.float32)
    for k in range(ids.shape[0]):
        weight = weight + jnp.where(ids[k : k + 1, :] == place_expert, gains[k : k + 1, :], 0.0)
    first = weight.astype(jnp.bfloat16).astype(jnp.float32)
    second = (weight - first).astype(jnp.bfloat16).astype(jnp.float32)
    third = weight - first - second
    packed = jnp.where(
        place_term == 0,
        first,
        jnp.where(place_term == 1, second, jnp.where(place_term == 2, third, 0.0)),
    )
    tok[0, 0, :, width:] = packed.T.astype(jnp.bfloat16)

    loads[2].wait()
    pl.semaphore_wait(barrier, 3)
    tok_copy(0, 0).start()
    tok_copy(0, 1).start()
    pair_copy(0).start()

    rs_recv[0] = jnp.zeros(rs_recv.shape[1:], rs_recv.dtype)
    rs_recv[1] = jnp.zeros(rs_recv.shape[1:], rs_recv.dtype)

    bits = lax.broadcasted_iota(jnp.int32, (ROT, ROT), 0) & lax.broadcasted_iota(jnp.int32, (ROT, ROT), 1)
    bits = bits ^ (bits >> 4)
    bits = bits ^ (bits >> 2)
    bits = (bits ^ (bits >> 1)) & 1
    signs = (1 - 2 * bits).astype(jnp.float32).astype(jnp.bfloat16)
    norm = 1.0 / math.sqrt(ROT)

    loads[3].wait()
    for which in range(2):
        start = jnp.where(which == 0, core, 1 - core) * half
        for block in range(half // ROT):
            columns = pl.ds(pl.multiple_of(start + block * ROT, ROT), ROT)
            turned = jnp.dot(wd_raw[:, columns], signs, preferred_element_type=jnp.float32) * norm
            wd[which, :, block * ROT : (block + 1) * ROT] = turned.astype(jnp.bfloat16)
    loads[4].wait()
    loads[5].wait()

    def step(s, carry):
        pair_copy(s).wait_recv()
        x = tok[s, :, :, :width].reshape(2 * rows, width)
        gate = jnp.dot(x, wg[...], preferred_element_type=jnp.float32)
        up = jnp.dot(x, wu[...], preferred_element_type=jnp.float32)
        hidden = (gate / (1.0 + jnp.exp(-gate)) * up).astype(jnp.bfloat16)

        @pl.when(s < last)
        def _():
            tok_copy(s, 0).wait_recv()
            tok_copy(s, 1).wait_recv()

            @pl.when(s + 1 < last)
            def _():
                tok_copy(s + 1, 0).start()
                tok_copy(s + 1, 1).start()

            pair_copy(s + 1).start()

        theirs = jnp.dot(hidden, wd[1], preferred_element_type=jnp.float32).astype(jnp.bfloat16)
        exch_send[s, :rows] = theirs[rows:]
        exch_send[s, rows:] = theirs[:rows]
        exch_copy(s).start()
        mine[...] = jnp.dot(hidden, wd[0], preferred_element_type=jnp.float32)
        tail = tok[s, :, :, width:].reshape(2 * rows, ROT).astype(jnp.float32)
        wide = lax.broadcasted_iota(jnp.int32, (2 * rows, ROT), 1)
        gain = jnp.sum(jnp.where(lax.rem(wide, slots) == expert, tail, 0.0), axis=1, keepdims=True)
        exch_copy(s).wait_recv()

        for block in range(half // ROT):
            columns = slice(block * ROT, (block + 1) * ROT)
            value = mine[:, columns] + exch_recv[s, :, columns].astype(jnp.float32)
            scale = jnp.max(jnp.abs(value), axis=1, keepdims=True) + 1e-06
            quantized = (value * (1.0 / scale) + 3.0).astype(jnp.bfloat16)
            mine[:, columns] = (quantized.astype(jnp.float32) - 3.0) * (scale * gain)

        for piece in range(pieces):
            for way in range(2):
                @pl.when(s >= 2)
                def _():
                    rs_copy(s - 1, way, piece).wait_recv()

                for which in range(2):
                    top = which * rows + way * half_rows
                    total = mine[top : top + half_rows, piece * part : (piece + 1) * part]
                    total = total + rs_recv[s, way, piece, which].astype(jnp.float32)
                    rs_send[s, way, piece, which] = total.astype(jnp.bfloat16)

                @pl.when(s >= 1)
                def _():
                    rs_copy(s, way, piece).start()

        return carry

    lax.fori_loop(0, slots, step, 0)

    doubled = jnp.concatenate([signs, signs], axis=0)
    for piece in range(pieces):
        for way in range(2):
            rs_copy(last, way, piece).wait_recv()
        for which in (1, 0):
            for block in range(part // ROT):
                inner = slice(block * ROT, (block + 1) * ROT)
                start = piece * part + block * ROT
                sums = [
                    rs_send[0, way, piece, which, :, inner].astype(jnp.float32)
                    + rs_recv[slots, way, piece, which, :, inner].astype(jnp.float32)
                    for way in range(2)
                ]
                total = jnp.concatenate(sums, axis=0)
                high = total.astype(jnp.bfloat16)
                low = (total - high.astype(jnp.float32)).astype(jnp.bfloat16)
                turned = jnp.dot(
                    jnp.concatenate([high, low], axis=1), doubled, preferred_element_type=jnp.float32
                )
                result = (turned * norm).astype(jnp.bfloat16)
                if which == 1:
                    fin_send[piece, :, inner] = result
                else:
                    out_ref[:, pl.ds(pl.multiple_of(core * half + start, ROT), ROT)] = result
            if which == 1:
                fin_copy(piece).start()

    def drain(s, carry):
        pair_copy(s).wait_send()
        exch_copy(s).wait_send()
        for way in range(2):
            @pl.when(s < last)
            def _():
                tok_copy(s, way).wait_send()

            @pl.when(s >= 1)
            def _():
                for piece in range(pieces):
                    rs_copy(s, way, piece).wait_send()
        return carry

    lax.fori_loop(0, slots, drain, 0)
    for piece in range(pieces):
        fin_copy(piece).wait_recv()
        start = (1 - core) * half + piece * part
        out_ref[:, pl.ds(pl.multiple_of(start, part), part)] = fin_recv[piece]
        fin_copy(piece).wait_send()


def ring_layer(tokens, expert_ids, gate_weights, w_gate, w_up, w_down):
    rows, width = tokens.shape
    hidden = w_gate.shape[2]
    half = width // 2
    slots = 2 * lax.axis_size("expert")
    pieces = PIECES
    dma, bf16 = pltpu.SemaphoreType.DMA, jnp.bfloat16
    anywhere = pl.BlockSpec(memory_space=pl.ANY)
    vmem = pl.BlockSpec(memory_space=pltpu.VMEM)
    return pl.pallas_call(
        ring_kernel,
        out_shape=jax.ShapeDtypeStruct((rows, width), bf16),
        in_specs=[anywhere] * 6,
        out_specs=vmem,
        scratch_shapes=[
            pltpu.VMEM((slots, 2, rows, width + ROT), bf16),
            pltpu.VMEM((width, hidden), bf16),
            pltpu.VMEM((width, hidden), bf16),
            pltpu.VMEM((hidden, width), bf16),
            pltpu.VMEM((2, hidden, half), bf16),
            pltpu.VMEM((2 * rows, half), jnp.float32),
            pltpu.VMEM((slots, 2 * rows, half), bf16),
            pltpu.VMEM((slots, 2 * rows, half), bf16),
            pltpu.VMEM((slots, 2, pieces, 2, rows // 2, half // pieces), bf16),
            pltpu.VMEM((slots + 1, 2, pieces, 2, rows // 2, half // pieces), bf16),
            pltpu.VMEM((pieces, rows, half // pieces), bf16),
            pltpu.VMEM((pieces, rows, half // pieces), bf16),
            pltpu.VMEM((expert_ids.shape[1], rows), jnp.int32),
            pltpu.VMEM((expert_ids.shape[1], rows), jnp.float32),
            dma((6,)),
            dma((2, slots)),
            dma((2, slots)),
            dma((slots,)),
            dma((slots,)),
            dma((slots,)),
            dma((slots,)),
            dma((2, pieces, slots)),
            dma((2, pieces, slots + 1)),
            dma((2, pieces)),
        ],
        compiler_params=pltpu.CompilerParams(
            collective_id=0, has_side_effects=True, vmem_limit_bytes=56 * 1024 * 1024
        ),
    )(tokens, expert_ids.T, gate_weights.T, w_gate, w_up, w_down)


def local(tokens, expert_ids, gate_weights, w_gate, w_up, w_down):
    hadamard_table = hadamard()
    tok_rows, model_width = tokens.shape
    top_count = expert_ids.shape[1]
    n_expert = lax.axis_size("expert")
    n_tensor = lax.axis_size("tensor")
    devices = n_expert * n_tensor
    experts = devices // 2
    capacity = max(2, min(tok_rows, 5 * tok_rows * top_count // (4 * experts)))
    if capacity == tok_rows and n_tensor == 4 and experts == 2 * n_expert and experts * 3 <= ROT:
        return ring_layer(tokens, expert_ids, gate_weights, w_gate, w_up, w_down)
    half_width = model_width // 2
    my_half = lax.axis_index("tensor") % 2
    gate_mat = w_gate[0]
    up_mat = w_up[0]
    down_mat = w_down[0]
    flat_ids = expert_ids.reshape(-1)
    onehot = (flat_ids[:, None] == lax.iota(jnp.int32, experts)[None, :]).astype(jnp.int32)
    slot_index = jnp.sum((jnp.cumsum(onehot, axis=0, dtype=jnp.int32) - onehot) * onehot, axis=1)
    lower_row = 2 * flat_ids * capacity + slot_index
    upper_row = lower_row + capacity
    copies = tokens[lax.iota(jnp.int32, tok_rows * top_count) // top_count]
    both_rows = jnp.concatenate([lower_row, upper_row])
    outgoing = jnp.zeros((devices * capacity, model_width), jnp.bfloat16)
    outgoing = outgoing.at[both_rows].set(jnp.concatenate([copies, copies], axis=0))
    received = lax.all_to_all(
        outgoing.reshape(devices, capacity, model_width),
        ("expert", "tensor"),
        split_axis=0,
        concat_axis=0,
        tiled=True,
    )
    token_rows = received.reshape(-1, model_width)
    item_count = received.shape[1]
    gate_proj = jnp.dot(token_rows, gate_mat, preferred_element_type=jnp.float32)
    up_proj = jnp.dot(token_rows, up_mat, preferred_element_type=jnp.float32)
    hidden = (jax.nn.silu(gate_proj) * up_proj).astype(jnp.bfloat16)
    partial_out = jnp.dot(hidden, down_mat, preferred_element_type=jnp.float32)
    own_part = lax.dynamic_slice_in_dim(partial_out, my_half * half_width, half_width, 1)
    other_part = lax.dynamic_slice_in_dim(partial_out, (1 - my_half) * half_width, half_width, 1)
    partner_part = swapped(other_part.astype(jnp.bfloat16), "tensor", 0).astype(other_part.dtype)
    summed = own_part + partner_part
    rotated = rotate(summed, hadamard_table).reshape(-1, half_width // ROT, ROT)
    scales = jnp.max(jnp.abs(rotated), axis=-1) + 1e-06
    quantized = (rotated / scales[:, :, None] + 3.0).astype(jnp.bfloat16)
    quant_out = quantized.reshape(devices, item_count, half_width)
    scale_out = scales.reshape(devices, item_count, half_width // ROT)
    back_quant, back_scales = (
        lax.all_to_all(quant_out, ("expert", "tensor"), split_axis=0, concat_axis=0, tiled=True),
        lax.all_to_all(
            scale_out.astype(jnp.bfloat16),
            ("expert", "tensor"),
            split_axis=0,
            concat_axis=0,
            tiled=True,
        ).astype(scale_out.dtype),
    )
    flat_quant = back_quant.reshape(devices * capacity, half_width // ROT, ROT)
    flat_scales = back_scales.reshape(devices * capacity, half_width // ROT)

    def restore(row_index):
        picked = (flat_quant[row_index].astype(jnp.float32) - 3.0) * flat_scales[row_index][
            :, :, None
        ]
        return picked.reshape(-1, half_width)

    restored = jnp.concatenate([restore(lower_row), restore(upper_row)], axis=1)
    mixed = jnp.einsum(
        "tkd,tk->td",
        restored.reshape(tok_rows, top_count, model_width),
        gate_weights,
        precision=lax.Precision.HIGHEST,
    )
    return rotate(mixed, hadamard_table).astype(jnp.bfloat16)


def solution(mesh):
    in_specs = (
        P(("group", "expert", "tensor"), None),
        P(("group", "expert", "tensor"), None),
        P(("group", "expert", "tensor"), None),
        P(("expert", "tensor"), None, None),
        P(("expert", "tensor"), None, None),
        P(("expert", "tensor"), None, None),
    )
    out_specs = P(("group", "expert", "tensor"), None)
    return jax.shard_map(local, mesh=mesh, in_specs=in_specs, out_specs=out_specs, check_vma=False)
```

```python
import math

import jax
import jax.numpy as jnp
from jax import lax
from jax.experimental import pallas as pl
from jax.experimental.pallas import tpu as pltpu
from jax.sharding import PartitionSpec as P

ROT = 128


def swapped(value, axis, apart):
    mask = 2**apart
    pairs = [(source, source ^ mask) for source in range(lax.axis_size(axis))]
    return lax.ppermute(value, axis, pairs)


def hadamard():
    position = lax.iota(jnp.int32, ROT)
    common_bits = jnp.bitwise_and(position[:, None], position[None, :])
    parity = jnp.zeros((ROT, ROT), jnp.int32)
    for bit_index in range(ROT.bit_length() - 1):
        parity = parity + jnp.bitwise_and(jnp.right_shift(common_bits, bit_index), 1)
    return (1 - 2 * (parity % 2)).astype(jnp.float32) / math.sqrt(ROT)


def rotate(values, hadamard_table):
    blocks = values.reshape(values.shape[0], -1, ROT)
    turned = jnp.einsum("rbi,ij->rbj", blocks, hadamard_table, precision=lax.Precision.HIGHEST)
    return turned.reshape(values.shape)


PIECES = 4


def ring_kernel(
    tokens_ref, ids_ref, gains_ref, gate_ref, up_ref, down_ref, out_ref,
    tok, wg, wu, wd_raw, wd, mine, exch_send, exch_recv, rs_send, rs_recv, fin_send, fin_own,
    ids, gains, wt, load_sem, tok_send_sem, tok_recv_sem, pair_send_sem, pair_recv_sem,
    exch_send_sem, exch_recv_sem, rs_send_sem, rs_recv_sem, fin_sem,
    wt_send_sem, wt_recv_sem, wt_pair_send_sem, wt_pair_recv_sem,
):
    slots, _, rows, _ = tok.shape
    half_rows = rows // 2
    width = tokens_ref.shape[1]
    half = width // 2
    last = slots - 1
    hops = wt.shape[1] - 1
    pieces, part = rs_send.shape[2], rs_send.shape[5]

    group = lax.axis_index("group")
    along_z = lax.axis_index("expert")
    tensor = lax.axis_index("tensor")
    core = lax.rem(tensor, 2)
    along_x = tensor // 2
    length = slots // 2
    expert = along_z * 2 + along_x
    position = jnp.where(along_x == 0, along_z, slots - 1 - along_z)

    def device_at(place):
        place = lax.rem(place + slots, slots)
        x = place // length
        z = jnp.where(x == 0, place, slots - 1 - place)
        return (group, z, 2 * x + core)

    neighbours = (device_at(position + 1), device_at(position - 1))
    partner = (group, along_z, 2 * along_x + 1 - core)

    def remote(src, dst, send, recv, device):
        return pltpu.make_async_remote_copy(
            src_ref=src, dst_ref=dst, send_sem=send, recv_sem=recv,
            device_id=device, device_id_type=pl.DeviceIdType.MESH,
        )

    def tok_copy(s, way, src=None):
        mine_way = pl.ds(way * half_rows, half_rows)
        return remote(
            tok.at[s, 0, mine_way] if src is None else src.at[mine_way], tok.at[s + 1, 0, mine_way],
            tok_send_sem.at[way, s], tok_recv_sem.at[way, s + 1], neighbours[way],
        )

    def pair_copy(s, src=None):
        src = tok.at[s, 0] if src is None else src
        return remote(src, tok.at[s, 1], pair_send_sem.at[s], pair_recv_sem.at[s], partner)

    def exch_copy(s):
        return remote(
            exch_send.at[s], exch_recv.at[s], exch_send_sem.at[s], exch_recv_sem.at[s], partner
        )

    def rs_copy(s, way, piece):
        return remote(
            rs_send.at[s, way, piece], rs_recv.at[s + 1, way, piece],
            rs_send_sem.at[way, piece, s], rs_recv_sem.at[way, piece, s + 1], neighbours[way],
        )

    def wt_copy(s, way):
        return remote(
            wt.at[way, s, 0], wt.at[way, s + 1, 0],
            wt_send_sem.at[way, s], wt_recv_sem.at[way, s + 1], neighbours[way],
        )

    def wt_pair(s, way):
        return remote(
            wt.at[way, s, 0], wt.at[way, s, 1],
            wt_pair_send_sem.at[way, s], wt_pair_recv_sem.at[way, s], partner,
        )

    def fin_place(piece):
        start = core * half + piece * part
        return out_ref.at[:, pl.ds(pl.multiple_of(start, ROT), part)]

    def fin_copy(piece):
        return remote(
            fin_send.at[piece], fin_place(piece), fin_sem.at[0, piece], fin_sem.at[1, piece], partner
        )

    def keep_copy(piece):
        return pltpu.make_async_copy(fin_own.at[piece], fin_place(piece), fin_sem.at[2, piece])

    barrier = pltpu.get_barrier_semaphore()
    for device in (*neighbours, partner):
        pl.semaphore_signal(barrier, inc=1, device_id=device, device_id_type=pl.DeviceIdType.MESH)

    loads = [
        pltpu.make_async_copy(tokens_ref, tok.at[0, 0], load_sem.at[0]),
        pltpu.make_async_copy(down_ref.at[0], wd_raw, load_sem.at[1]),
        pltpu.make_async_copy(gate_ref.at[0], wg, load_sem.at[2]),
        pltpu.make_async_copy(up_ref.at[0], wu, load_sem.at[3]),
        pltpu.make_async_copy(ids_ref, ids, load_sem.at[4]),
        pltpu.make_async_copy(gains_ref, gains, load_sem.at[5]),
    ]
    loads = loads[4:] + loads[:4]
    for load in loads:
        load.start()

    pl.semaphore_wait(barrier, 3)
    tok_copy(0, 0, tokens_ref).start()
    tok_copy(0, 1, tokens_ref).start()
    pair_copy(0, tokens_ref).start()

    loads[0].wait()
    loads[1].wait()
    named = lax.broadcasted_iota(jnp.int32, (slots, rows), 0)
    weight = jnp.zeros((slots, rows), jnp.float32)
    for k in range(ids.shape[0]):
        weight = weight + jnp.where(ids[k : k + 1, :] == named, gains[k : k + 1, :], 0.0)
    weight = jnp.concatenate([weight, weight], axis=1)
    for way in range(2):
        wt[way, 0, 0] = weight
    for way in range(2):
        wt_copy(0, way).start()
        wt_pair(0, way).start()

    rs_recv[0] = jnp.zeros(rs_recv.shape[1:], rs_recv.dtype)
    rs_recv[1] = jnp.zeros(rs_recv.shape[1:], rs_recv.dtype)

    bits = lax.broadcasted_iota(jnp.int32, (ROT, ROT), 0) & lax.broadcasted_iota(jnp.int32, (ROT, ROT), 1)
    bits = bits ^ (bits >> 4)
    bits = bits ^ (bits >> 2)
    bits = (bits ^ (bits >> 1)) & 1
    signs = (1 - 2 * bits).astype(jnp.float32).astype(jnp.bfloat16)
    norm = 1.0 / math.sqrt(ROT)

    loads[3].wait()
    for which in range(2):
        start = jnp.where(which == 0, core, 1 - core) * half
        for block in range(half // ROT):
            columns = pl.ds(pl.multiple_of(start + block * ROT, ROT), ROT)
            turned = jnp.dot(wd_raw[:, columns], signs, preferred_element_type=jnp.float32) * norm
            wd[which, :, block * ROT : (block + 1) * ROT] = turned.astype(jnp.bfloat16)
    loads[2].wait()
    loads[4].wait()
    loads[5].wait()

    def step(s, carry):
        pair_copy(s).wait_recv()
        x = tok[s].reshape(2 * rows, width)
        gate = jnp.dot(x, wg[...], preferred_element_type=jnp.float32)
        up = jnp.dot(x, wu[...], preferred_element_type=jnp.float32)
        hidden = (gate / (1.0 + jnp.exp(-gate)) * up).astype(jnp.bfloat16)

        @pl.when(s < last)
        def _():
            for way in range(2):
                tok_copy(s, way).wait_recv()

                @pl.when(s + 1 < last)
                def _():
                    tok_copy(s + 1, way).start()

            pair_copy(s + 1).start()

        @pl.when(s < hops)
        def _():
            for way in range(2):
                wt_copy(s, way).wait_recv()

                @pl.when(s + 1 < hops)
                def _():
                    wt_copy(s + 1, way).start()

                wt_pair(s + 1, way).start()

        theirs = jnp.dot(hidden, wd[1], preferred_element_type=jnp.float32).astype(jnp.bfloat16)
        exch_send[s, :rows] = theirs[rows:]
        exch_send[s, rows:] = theirs[:rows]
        exch_copy(s).start()
        mine[...] = jnp.dot(hidden, wd[0], preferred_element_type=jnp.float32)

        @pl.when(s <= hops)
        def _():
            for way in range(2):
                wt_pair(s, way).wait_recv()

        near = s <= hops
        apart = jnp.where(near, s, slots - s)
        behind = jnp.where(near, 0, 1)
        lane = lax.broadcasted_iota(jnp.int32, (slots, 2 * rows), 1)
        backward = lax.rem(lane, rows) >= half_rows
        own = jnp.where(backward, wt[1 - behind, apart, 0], wt[behind, apart, 0])
        other = jnp.where(backward, wt[1 - behind, apart, 1], wt[behind, apart, 1])
        row = lax.broadcasted_iota(jnp.int32, (slots, 2 * rows), 0)
        chosen = jnp.where(row == expert, jnp.where(lane < rows, own, other), 0.0)
        chosen = jnp.sum(chosen, axis=0, keepdims=True)
        diagonal = lax.broadcasted_iota(jnp.int32, (2 * rows, 2 * rows), 0) == lax.broadcasted_iota(
            jnp.int32, (2 * rows, 2 * rows), 1
        )
        gain = jnp.sum(jnp.where(diagonal, chosen, 0.0), axis=1, keepdims=True)
        exch_copy(s).wait_recv()

        for block in range(half // ROT):
            columns = slice(block * ROT, (block + 1) * ROT)
            value = mine[:, columns] + exch_recv[s, :, columns].astype(jnp.float32)
            scale = jnp.max(jnp.abs(value), axis=1, keepdims=True) + 1e-06
            quantized = (value * (1.0 / scale) + 3.0).astype(jnp.bfloat16)
            mine[:, columns] = (quantized.astype(jnp.float32) - 3.0) * (scale * gain)

        for piece in range(pieces):
            for way in range(2):
                @pl.when(s >= 2)
                def _():
                    rs_copy(s - 1, way, piece).wait_recv()

                for which in range(2):
                    top = which * rows + way * half_rows
                    total = mine[top : top + half_rows, piece * part : (piece + 1) * part]
                    total = total + rs_recv[s, way, piece, which].astype(jnp.float32)
                    rs_send[s, way, piece, which] = total.astype(jnp.bfloat16)

                @pl.when(s >= 1)
                def _():
                    rs_copy(s, way, piece).start()

        return carry

    lax.fori_loop(0, slots, step, 0)

    doubled = jnp.concatenate([signs, signs], axis=0)
    for piece in range(pieces):
        for way in range(2):
            rs_copy(last, way, piece).wait_recv()
        for which in (1, 0):
            for block in range(part // ROT):
                inner = slice(block * ROT, (block + 1) * ROT)
                sums = [
                    rs_send[0, way, piece, which, :, inner].astype(jnp.float32)
                    + rs_recv[slots, way, piece, which, :, inner].astype(jnp.float32)
                    for way in range(2)
                ]
                total = jnp.concatenate(sums, axis=0)
                high = total.astype(jnp.bfloat16)
                low = (total - high.astype(jnp.float32)).astype(jnp.bfloat16)
                turned = jnp.dot(
                    jnp.concatenate([high, low], axis=1), doubled, preferred_element_type=jnp.float32
                )
                result = (turned * norm).astype(jnp.bfloat16)
                if which == 1:
                    fin_send[piece, :, inner] = result
                else:
                    fin_own[piece, :, inner] = result
            if which == 1:
                fin_copy(piece).start()
            else:
                keep_copy(piece).start()

    def drain(s, carry):
        pair_copy(s).wait_send()
        exch_copy(s).wait_send()
        for way in range(2):
            @pl.when(s < hops)
            def _():
                wt_copy(s, way).wait_send()

            @pl.when(s <= hops)
            def _():
                wt_pair(s, way).wait_send()

            @pl.when(s < last)
            def _():
                tok_copy(s, way).wait_send()

            @pl.when(s >= 1)
            def _():
                for piece in range(pieces):
                    rs_copy(s, way, piece).wait_send()
        return carry

    lax.fori_loop(0, slots, drain, 0)
    for piece in range(pieces):
        fin_copy(piece).wait_recv()
        keep_copy(piece).wait()
        fin_copy(piece).wait_send()


def ring_layer(tokens, expert_ids, gate_weights, w_gate, w_up, w_down):
    rows, width = tokens.shape
    hidden = w_gate.shape[2]
    half = width // 2
    slots = 2 * lax.axis_size("expert")
    pieces, hops = PIECES, slots // 2
    dma, bf16 = pltpu.SemaphoreType.DMA, jnp.bfloat16
    anywhere = pl.BlockSpec(memory_space=pl.ANY)
    return pl.pallas_call(
        ring_kernel,
        out_shape=jax.ShapeDtypeStruct((rows, width), bf16),
        in_specs=[anywhere] * 6,
        out_specs=anywhere,
        scratch_shapes=[
            pltpu.VMEM((slots, 2, rows, width), bf16),
            pltpu.VMEM((width, hidden), bf16),
            pltpu.VMEM((width, hidden), bf16),
            pltpu.VMEM((hidden, width), bf16),
            pltpu.VMEM((2, hidden, half), bf16),
            pltpu.VMEM((2 * rows, half), jnp.float32),
            pltpu.VMEM((slots, 2 * rows, half), bf16),
            pltpu.VMEM((slots, 2 * rows, half), bf16),
            pltpu.VMEM((slots, 2, pieces, 2, rows // 2, half // pieces), bf16),
            pltpu.VMEM((slots + 1, 2, pieces, 2, rows // 2, half // pieces), bf16),
            pltpu.VMEM((pieces, rows, half // pieces), bf16),
            pltpu.VMEM((pieces, rows, half // pieces), bf16),
            pltpu.VMEM((expert_ids.shape[1], rows), jnp.int32),
            pltpu.VMEM((expert_ids.shape[1], rows), jnp.float32),
            pltpu.VMEM((2, hops + 1, 2, slots, 2 * rows), jnp.float32),
            dma((6,)),
            dma((2, slots)),
            dma((2, slots)),
            dma((slots,)),
            dma((slots,)),
            dma((slots,)),
            dma((slots,)),
            dma((2, pieces, slots)),
            dma((2, pieces, slots + 1)),
            dma((3, pieces)),
            dma((2, hops + 1)),
            dma((2, hops + 1)),
            dma((2, hops + 1)),
            dma((2, hops + 1)),
        ],
        compiler_params=pltpu.CompilerParams(
            collective_id=0, has_side_effects=True, vmem_limit_bytes=56 * 1024 * 1024
        ),
    )(tokens, expert_ids.T, gate_weights.T, w_gate, w_up, w_down)


def local(tokens, expert_ids, gate_weights, w_gate, w_up, w_down):
    hadamard_table = hadamard()
    tok_rows, model_width = tokens.shape
    top_count = expert_ids.shape[1]
    n_expert = lax.axis_size("expert")
    n_tensor = lax.axis_size("tensor")
    devices = n_expert * n_tensor
    experts = devices // 2
    capacity = max(2, min(tok_rows, 5 * tok_rows * top_count // (4 * experts)))
    if capacity == tok_rows and n_tensor == 4 and experts == 2 * n_expert and 2 * tok_rows == ROT:
        return ring_layer(tokens, expert_ids, gate_weights, w_gate, w_up, w_down)
    half_width = model_width // 2
    my_half = lax.axis_index("tensor") % 2
    gate_mat = w_gate[0]
    up_mat = w_up[0]
    down_mat = w_down[0]
    flat_ids = expert_ids.reshape(-1)
    onehot = (flat_ids[:, None] == lax.iota(jnp.int32, experts)[None, :]).astype(jnp.int32)
    slot_index = jnp.sum((jnp.cumsum(onehot, axis=0, dtype=jnp.int32) - onehot) * onehot, axis=1)
    lower_row = 2 * flat_ids * capacity + slot_index
    upper_row = lower_row + capacity
    copies = tokens[lax.iota(jnp.int32, tok_rows * top_count) // top_count]
    both_rows = jnp.concatenate([lower_row, upper_row])
    outgoing = jnp.zeros((devices * capacity, model_width), jnp.bfloat16)
    outgoing = outgoing.at[both_rows].set(jnp.concatenate([copies, copies], axis=0))
    received = lax.all_to_all(
        outgoing.reshape(devices, capacity, model_width),
        ("expert", "tensor"),
        split_axis=0,
        concat_axis=0,
        tiled=True,
    )
    token_rows = received.reshape(-1, model_width)
    item_count = received.shape[1]
    gate_proj = jnp.dot(token_rows, gate_mat, preferred_element_type=jnp.float32)
    up_proj = jnp.dot(token_rows, up_mat, preferred_element_type=jnp.float32)
    hidden = (jax.nn.silu(gate_proj) * up_proj).astype(jnp.bfloat16)
    partial_out = jnp.dot(hidden, down_mat, preferred_element_type=jnp.float32)
    own_part = lax.dynamic_slice_in_dim(partial_out, my_half * half_width, half_width, 1)
    other_part = lax.dynamic_slice_in_dim(partial_out, (1 - my_half) * half_width, half_width, 1)
    partner_part = swapped(other_part.astype(jnp.bfloat16), "tensor", 0).astype(other_part.dtype)
    summed = own_part + partner_part
    rotated = rotate(summed, hadamard_table).reshape(-1, half_width // ROT, ROT)
    scales = jnp.max(jnp.abs(rotated), axis=-1) + 1e-06
    quantized = (rotated / scales[:, :, None] + 3.0).astype(jnp.bfloat16)
    quant_out = quantized.reshape(devices, item_count, half_width)
    scale_out = scales.reshape(devices, item_count, half_width // ROT)
    back_quant, back_scales = (
        lax.all_to_all(quant_out, ("expert", "tensor"), split_axis=0, concat_axis=0, tiled=True),
        lax.all_to_all(
            scale_out.astype(jnp.bfloat16),
            ("expert", "tensor"),
            split_axis=0,
            concat_axis=0,
            tiled=True,
        ).astype(scale_out.dtype),
    )
    flat_quant = back_quant.reshape(devices * capacity, half_width // ROT, ROT)
    flat_scales = back_scales.reshape(devices * capacity, half_width // ROT)

    def restore(row_index):
        picked = (flat_quant[row_index].astype(jnp.float32) - 3.0) * flat_scales[row_index][
            :, :, None
        ]
        return picked.reshape(-1, half_width)

    restored = jnp.concatenate([restore(lower_row), restore(upper_row)], axis=1)
    mixed = jnp.einsum(
        "tkd,tk->td",
        restored.reshape(tok_rows, top_count, model_width),
        gate_weights,
        precision=lax.Precision.HIGHEST,
    )
    return rotate(mixed, hadamard_table).astype(jnp.bfloat16)


def solution(mesh):
    in_specs = (
        P(("group", "expert", "tensor"), None),
        P(("group", "expert", "tensor"), None),
        P(("group", "expert", "tensor"), None),
        P(("expert", "tensor"), None, None),
        P(("expert", "tensor"), None, None),
        P(("expert", "tensor"), None, None),
    )
    out_specs = P(("group", "expert", "tensor"), None)
    return jax.shard_map(local, mesh=mesh, in_specs=in_specs, out_specs=out_specs, check_vma=False)
```

```python
import math

import jax
import jax.numpy as jnp
from jax import lax
from jax.experimental import pallas as pl
from jax.experimental.pallas import tpu as pltpu
from jax.sharding import PartitionSpec as P

ROT = 128


def swapped(value, axis, apart):
    mask = 2**apart
    pairs = [(source, source ^ mask) for source in range(lax.axis_size(axis))]
    return lax.ppermute(value, axis, pairs)


def hadamard():
    position = lax.iota(jnp.int32, ROT)
    common_bits = jnp.bitwise_and(position[:, None], position[None, :])
    parity = jnp.zeros((ROT, ROT), jnp.int32)
    for bit_index in range(ROT.bit_length() - 1):
        parity = parity + jnp.bitwise_and(jnp.right_shift(common_bits, bit_index), 1)
    return (1 - 2 * (parity % 2)).astype(jnp.float32) / math.sqrt(ROT)


def rotate(values, hadamard_table):
    blocks = values.reshape(values.shape[0], -1, ROT)
    turned = jnp.einsum("rbi,ij->rbj", blocks, hadamard_table, precision=lax.Precision.HIGHEST)
    return turned.reshape(values.shape)


PIECES = 4


def ring_kernel(
    tokens_ref, ids_ref, gains_ref, gate_ref, up_ref, down_ref, out_ref,
    tok, wg, wu, wd_raw, wd, mine, exch_send, exch_recv, rs_send, rs_recv, fin_send, fin_own,
    ids, gains, wt, load_sem, tok_send_sem, tok_recv_sem, pair_send_sem, pair_recv_sem,
    exch_send_sem, exch_recv_sem, rs_send_sem, rs_recv_sem, fin_sem,
    wt_send_sem, wt_recv_sem, wt_pair_send_sem, wt_pair_recv_sem,
):
    slots, _, rows, _ = tok.shape
    half_rows = rows // 2
    width = tokens_ref.shape[1]
    half = width // 2
    last = slots - 1
    hops = wt.shape[1] - 1
    pieces, part = rs_send.shape[2], rs_send.shape[5]

    group = lax.axis_index("group")
    along_z = lax.axis_index("expert")
    tensor = lax.axis_index("tensor")
    core = lax.rem(tensor, 2)
    along_x = tensor // 2
    length = slots // 2
    expert = along_z * 2 + along_x
    position = jnp.where(along_x == 0, along_z, slots - 1 - along_z)

    def device_at(place):
        place = lax.rem(place + slots, slots)
        x = place // length
        z = jnp.where(x == 0, place, slots - 1 - place)
        return (group, z, 2 * x + core)

    neighbours = (device_at(position + 1), device_at(position - 1))
    partner = (group, along_z, 2 * along_x + 1 - core)

    def remote(src, dst, send, recv, device):
        return pltpu.make_async_remote_copy(
            src_ref=src, dst_ref=dst, send_sem=send, recv_sem=recv,
            device_id=device, device_id_type=pl.DeviceIdType.MESH,
        )

    def tok_copy(s, way, src=None):
        mine_way = pl.ds(way * half_rows, half_rows)
        return remote(
            tok.at[s, 0, mine_way] if src is None else src.at[mine_way], tok.at[s + 1, 0, mine_way],
            tok_send_sem.at[way, s], tok_recv_sem.at[way, s + 1], neighbours[way],
        )

    def pair_copy(s, src=None):
        src = tok.at[s, 0] if src is None else src
        return remote(src, tok.at[s, 1], pair_send_sem.at[s], pair_recv_sem.at[s], partner)

    def exch_copy(s):
        return remote(
            exch_send.at[s], exch_recv.at[s], exch_send_sem.at[s], exch_recv_sem.at[s], partner
        )

    def rs_copy(s, way, piece):
        return remote(
            rs_send.at[s, way, piece], rs_recv.at[s + 1, way, piece],
            rs_send_sem.at[way, piece, s], rs_recv_sem.at[way, piece, s + 1], neighbours[way],
        )

    def wt_copy(s, way):
        return remote(
            wt.at[way, s, 0], wt.at[way, s + 1, 0],
            wt_send_sem.at[way, s], wt_recv_sem.at[way, s + 1], neighbours[way],
        )

    def wt_pair(s, way):
        return remote(
            wt.at[way, s, 0], wt.at[way, s, 1],
            wt_pair_send_sem.at[way, s], wt_pair_recv_sem.at[way, s], partner,
        )

    def fin_place(piece):
        start = core * half + piece * part
        return out_ref.at[:, pl.ds(pl.multiple_of(start, ROT), part)]

    def fin_copy(piece):
        return remote(
            fin_send.at[piece], fin_place(piece), fin_sem.at[0, piece], fin_sem.at[1, piece], partner
        )

    def keep_copy(piece):
        return pltpu.make_async_copy(fin_own.at[piece], fin_place(piece), fin_sem.at[2, piece])

    barrier = pltpu.get_barrier_semaphore()
    for device in (*neighbours, partner):
        pl.semaphore_signal(barrier, inc=1, device_id=device, device_id_type=pl.DeviceIdType.MESH)

    loads = [
        pltpu.make_async_copy(tokens_ref, tok.at[0, 0], load_sem.at[0]),
        pltpu.make_async_copy(down_ref.at[0], wd_raw, load_sem.at[1]),
        pltpu.make_async_copy(gate_ref.at[0], wg, load_sem.at[2]),
        pltpu.make_async_copy(up_ref.at[0], wu, load_sem.at[3]),
        pltpu.make_async_copy(ids_ref, ids, load_sem.at[4]),
        pltpu.make_async_copy(gains_ref, gains, load_sem.at[5]),
    ]
    loads = loads[4:] + loads[:4]
    for load in loads:
        load.start()

    pl.semaphore_wait(barrier, 3)
    tok_copy(0, 0, tokens_ref).start()
    tok_copy(0, 1, tokens_ref).start()
    pair_copy(0, tokens_ref).start()

    loads[0].wait()
    loads[1].wait()
    named = lax.broadcasted_iota(jnp.int32, (slots, rows), 0)
    weight = jnp.zeros((slots, rows), jnp.float32)
    for k in range(ids.shape[0]):
        weight = weight + jnp.where(ids[k : k + 1, :] == named, gains[k : k + 1, :], 0.0)
    weight = jnp.concatenate([weight, weight], axis=1)
    for way in range(2):
        wt[way, 0, 0] = weight
    for way in range(2):
        wt_copy(0, way).start()
        wt_pair(0, way).start()

    rs_recv[0] = jnp.zeros(rs_recv.shape[1:], rs_recv.dtype)
    rs_recv[1] = jnp.zeros(rs_recv.shape[1:], rs_recv.dtype)

    bits = lax.broadcasted_iota(jnp.int32, (ROT, ROT), 0) & lax.broadcasted_iota(jnp.int32, (ROT, ROT), 1)
    bits = bits ^ (bits >> 4)
    bits = bits ^ (bits >> 2)
    bits = (bits ^ (bits >> 1)) & 1
    signs = (1 - 2 * bits).astype(jnp.float32).astype(jnp.bfloat16)
    norm = 1.0 / math.sqrt(ROT)

    loads[3].wait()
    for which in range(2):
        start = jnp.where(which == 0, core, 1 - core) * half
        for block in range(half // ROT):
            columns = pl.ds(pl.multiple_of(start + block * ROT, ROT), ROT)
            turned = jnp.dot(wd_raw[:, columns], signs, preferred_element_type=jnp.float32) * norm
            wd[which, :, block * ROT : (block + 1) * ROT] = turned.astype(jnp.bfloat16)
    loads[2].wait()
    loads[4].wait()
    loads[5].wait()

    def step(s, carry):
        pair_copy(s).wait_recv()
        x = tok[s].reshape(2 * rows, width)
        gate = jnp.dot(x, wg[...], preferred_element_type=jnp.float32)
        up = jnp.dot(x, wu[...], preferred_element_type=jnp.float32)
        hidden = (gate / (1.0 + jnp.exp(-gate)) * up).astype(jnp.bfloat16)

        @pl.when(s < last)
        def _():
            for way in range(2):
                tok_copy(s, way).wait_recv()

                @pl.when(s + 1 < last)
                def _():
                    tok_copy(s + 1, way).start()

            pair_copy(s + 1).start()

        @pl.when(s < hops)
        def _():
            for way in range(2):
                wt_copy(s, way).wait_recv()

                @pl.when(s + 1 < hops)
                def _():
                    wt_copy(s + 1, way).start()

                wt_pair(s + 1, way).start()

        theirs = jnp.dot(hidden, wd[1], preferred_element_type=jnp.float32).astype(jnp.bfloat16)
        exch_send[s, :rows] = theirs[rows:]
        exch_send[s, rows:] = theirs[:rows]
        exch_copy(s).start()
        mine[...] = jnp.dot(hidden, wd[0], preferred_element_type=jnp.float32)

        @pl.when(s <= hops)
        def _():
            for way in range(2):
                wt_pair(s, way).wait_recv()

        near = s <= hops
        apart = jnp.where(near, s, slots - s)
        behind = jnp.where(near, 0, 1)
        lane = lax.broadcasted_iota(jnp.int32, (slots, 2 * rows), 1)
        backward = lax.rem(lane, rows) >= half_rows
        own = jnp.where(backward, wt[1 - behind, apart, 0], wt[behind, apart, 0])
        other = jnp.where(backward, wt[1 - behind, apart, 1], wt[behind, apart, 1])
        row = lax.broadcasted_iota(jnp.int32, (slots, 2 * rows), 0)
        chosen = jnp.where(row == expert, jnp.where(lane < rows, own, other), 0.0)
        chosen = jnp.sum(chosen, axis=0, keepdims=True)
        diagonal = lax.broadcasted_iota(jnp.int32, (2 * rows, 2 * rows), 0) == lax.broadcasted_iota(
            jnp.int32, (2 * rows, 2 * rows), 1
        )
        gain = jnp.sum(jnp.where(diagonal, chosen, 0.0), axis=1, keepdims=True)
        exch_copy(s).wait_recv()

        for piece in range(pieces):
            for block in range(piece * part // ROT, (piece + 1) * part // ROT):
                columns = slice(block * ROT, (block + 1) * ROT)
                value = mine[:, columns] + exch_recv[s, :, columns].astype(jnp.float32)
                scale = jnp.max(jnp.abs(value), axis=1, keepdims=True) + 1e-06
                quantized = (value * (1.0 / scale) + 3.0).astype(jnp.bfloat16)
                mine[:, columns] = (quantized.astype(jnp.float32) - 3.0) * (scale * gain)

            for way in range(2):
                @pl.when(s >= 2)
                def _():
                    rs_copy(s - 1, way, piece).wait_recv()

                for which in range(2):
                    top = which * rows + way * half_rows
                    total = mine[top : top + half_rows, piece * part : (piece + 1) * part]
                    total = total + rs_recv[s, way, piece, which].astype(jnp.float32)
                    rs_send[s, way, piece, which] = total.astype(jnp.bfloat16)

                @pl.when(s >= 1)
                def _():
                    rs_copy(s, way, piece).start()

        return carry

    lax.fori_loop(0, slots, step, 0)

    doubled = jnp.concatenate([signs, signs], axis=0)
    for piece in range(pieces):
        for way in range(2):
            rs_copy(last, way, piece).wait_recv()
        for which in (1, 0):
            for block in range(part // ROT):
                inner = slice(block * ROT, (block + 1) * ROT)
                sums = [
                    rs_send[0, way, piece, which, :, inner].astype(jnp.float32)
                    + rs_recv[slots, way, piece, which, :, inner].astype(jnp.float32)
                    for way in range(2)
                ]
                total = jnp.concatenate(sums, axis=0)
                high = total.astype(jnp.bfloat16)
                low = (total - high.astype(jnp.float32)).astype(jnp.bfloat16)
                turned = jnp.dot(
                    jnp.concatenate([high, low], axis=1), doubled, preferred_element_type=jnp.float32
                )
                result = (turned * norm).astype(jnp.bfloat16)
                if which == 1:
                    fin_send[piece, :, inner] = result
                else:
                    fin_own[piece, :, inner] = result
            if which == 1:
                fin_copy(piece).start()
            else:
                keep_copy(piece).start()

    def drain(s, carry):
        pair_copy(s).wait_send()
        exch_copy(s).wait_send()
        for way in range(2):
            @pl.when(s < hops)
            def _():
                wt_copy(s, way).wait_send()

            @pl.when(s <= hops)
            def _():
                wt_pair(s, way).wait_send()

            @pl.when(s < last)
            def _():
                tok_copy(s, way).wait_send()

            @pl.when(s >= 1)
            def _():
                for piece in range(pieces):
                    rs_copy(s, way, piece).wait_send()
        return carry

    lax.fori_loop(0, slots, drain, 0)
    for piece in range(pieces):
        fin_copy(piece).wait_recv()
        keep_copy(piece).wait()
        fin_copy(piece).wait_send()


def ring_layer(tokens, expert_ids, gate_weights, w_gate, w_up, w_down):
    rows, width = tokens.shape
    hidden = w_gate.shape[2]
    half = width // 2
    slots = 2 * lax.axis_size("expert")
    pieces, hops = PIECES, slots // 2
    dma, bf16 = pltpu.SemaphoreType.DMA, jnp.bfloat16
    anywhere = pl.BlockSpec(memory_space=pl.ANY)
    return pl.pallas_call(
        ring_kernel,
        out_shape=jax.ShapeDtypeStruct((rows, width), bf16),
        in_specs=[anywhere] * 6,
        out_specs=anywhere,
        scratch_shapes=[
            pltpu.VMEM((slots, 2, rows, width), bf16),
            pltpu.VMEM((width, hidden), bf16),
            pltpu.VMEM((width, hidden), bf16),
            pltpu.VMEM((hidden, width), bf16),
            pltpu.VMEM((2, hidden, half), bf16),
            pltpu.VMEM((2 * rows, half), jnp.float32),
            pltpu.VMEM((slots, 2 * rows, half), bf16),
            pltpu.VMEM((slots, 2 * rows, half), bf16),
            pltpu.VMEM((slots, 2, pieces, 2, rows // 2, half // pieces), bf16),
            pltpu.VMEM((slots + 1, 2, pieces, 2, rows // 2, half // pieces), bf16),
            pltpu.VMEM((pieces, rows, half // pieces), bf16),
            pltpu.VMEM((pieces, rows, half // pieces), bf16),
            pltpu.VMEM((expert_ids.shape[1], rows), jnp.int32),
            pltpu.VMEM((expert_ids.shape[1], rows), jnp.float32),
            pltpu.VMEM((2, hops + 1, 2, slots, 2 * rows), jnp.float32),
            dma((6,)),
            dma((2, slots)),
            dma((2, slots)),
            dma((slots,)),
            dma((slots,)),
            dma((slots,)),
            dma((slots,)),
            dma((2, pieces, slots)),
            dma((2, pieces, slots + 1)),
            dma((3, pieces)),
            dma((2, hops + 1)),
            dma((2, hops + 1)),
            dma((2, hops + 1)),
            dma((2, hops + 1)),
        ],
        compiler_params=pltpu.CompilerParams(
            collective_id=0, has_side_effects=True, vmem_limit_bytes=56 * 1024 * 1024
        ),
    )(tokens, expert_ids.T, gate_weights.T, w_gate, w_up, w_down)


def local(tokens, expert_ids, gate_weights, w_gate, w_up, w_down):
    hadamard_table = hadamard()
    tok_rows, model_width = tokens.shape
    top_count = expert_ids.shape[1]
    n_expert = lax.axis_size("expert")
    n_tensor = lax.axis_size("tensor")
    devices = n_expert * n_tensor
    experts = devices // 2
    capacity = max(2, min(tok_rows, 5 * tok_rows * top_count // (4 * experts)))
    if capacity == tok_rows and n_tensor == 4 and experts == 2 * n_expert and 2 * tok_rows == ROT:
        return ring_layer(tokens, expert_ids, gate_weights, w_gate, w_up, w_down)
    half_width = model_width // 2
    my_half = lax.axis_index("tensor") % 2
    gate_mat = w_gate[0]
    up_mat = w_up[0]
    down_mat = w_down[0]
    flat_ids = expert_ids.reshape(-1)
    onehot = (flat_ids[:, None] == lax.iota(jnp.int32, experts)[None, :]).astype(jnp.int32)
    slot_index = jnp.sum((jnp.cumsum(onehot, axis=0, dtype=jnp.int32) - onehot) * onehot, axis=1)
    lower_row = 2 * flat_ids * capacity + slot_index
    upper_row = lower_row + capacity
    copies = tokens[lax.iota(jnp.int32, tok_rows * top_count) // top_count]
    both_rows = jnp.concatenate([lower_row, upper_row])
    outgoing = jnp.zeros((devices * capacity, model_width), jnp.bfloat16)
    outgoing = outgoing.at[both_rows].set(jnp.concatenate([copies, copies], axis=0))
    received = lax.all_to_all(
        outgoing.reshape(devices, capacity, model_width),
        ("expert", "tensor"),
        split_axis=0,
        concat_axis=0,
        tiled=True,
    )
    token_rows = received.reshape(-1, model_width)
    item_count = received.shape[1]
    gate_proj = jnp.dot(token_rows, gate_mat, preferred_element_type=jnp.float32)
    up_proj = jnp.dot(token_rows, up_mat, preferred_element_type=jnp.float32)
    hidden = (jax.nn.silu(gate_proj) * up_proj).astype(jnp.bfloat16)
    partial_out = jnp.dot(hidden, down_mat, preferred_element_type=jnp.float32)
    own_part = lax.dynamic_slice_in_dim(partial_out, my_half * half_width, half_width, 1)
    other_part = lax.dynamic_slice_in_dim(partial_out, (1 - my_half) * half_width, half_width, 1)
    partner_part = swapped(other_part.astype(jnp.bfloat16), "tensor", 0).astype(other_part.dtype)
    summed = own_part + partner_part
    rotated = rotate(summed, hadamard_table).reshape(-1, half_width // ROT, ROT)
    scales = jnp.max(jnp.abs(rotated), axis=-1) + 1e-06
    quantized = (rotated / scales[:, :, None] + 3.0).astype(jnp.bfloat16)
    quant_out = quantized.reshape(devices, item_count, half_width)
    scale_out = scales.reshape(devices, item_count, half_width // ROT)
    back_quant, back_scales = (
        lax.all_to_all(quant_out, ("expert", "tensor"), split_axis=0, concat_axis=0, tiled=True),
        lax.all_to_all(
            scale_out.astype(jnp.bfloat16),
            ("expert", "tensor"),
            split_axis=0,
            concat_axis=0,
            tiled=True,
        ).astype(scale_out.dtype),
    )
    flat_quant = back_quant.reshape(devices * capacity, half_width // ROT, ROT)
    flat_scales = back_scales.reshape(devices * capacity, half_width // ROT)

    def restore(row_index):
        picked = (flat_quant[row_index].astype(jnp.float32) - 3.0) * flat_scales[row_index][
            :, :, None
        ]
        return picked.reshape(-1, half_width)

    restored = jnp.concatenate([restore(lower_row), restore(upper_row)], axis=1)
    mixed = jnp.einsum(
        "tkd,tk->td",
        restored.reshape(tok_rows, top_count, model_width),
        gate_weights,
        precision=lax.Precision.HIGHEST,
    )
    return rotate(mixed, hadamard_table).astype(jnp.bfloat16)


def solution(mesh):
    in_specs = (
        P(("group", "expert", "tensor"), None),
        P(("group", "expert", "tensor"), None),
        P(("group", "expert", "tensor"), None),
        P(("expert", "tensor"), None, None),
        P(("expert", "tensor"), None, None),
        P(("expert", "tensor"), None, None),
    )
    out_specs = P(("group", "expert", "tensor"), None)
    return jax.shard_map(local, mesh=mesh, in_specs=in_specs, out_specs=out_specs, check_vma=False)
```
